128 devices in a mesh: sec: 4 (over z), dev: 32 (over x, y, core).
Axes of the slice: x: 4, y: 4, z: 4, core: 2. Of those that a mesh axis runs over, the one named last changes fastest.
Arguments:
- tokens: bfloat16 [4096, 3584], P(('sec', 'dev')), may hold values from -6 to 6
- expert_ids: int32 [4096, 8], P(('sec', 'dev')), may hold values from 0 to 127, all different within a row; in each aligned block of 32 rows (0 to 31, 32 to 63, ...) at most 4 rows name the same one
- gate_values: float32 [4096, 8], P(('sec', 'dev')), may hold values from 0.1 to 0.6
- w_gate: bfloat16 [128, 3584, 1024], P(('sec', 'dev')), may hold values from -0.09375 to 0.09375
- w_up: bfloat16 [128, 3584, 1024], P(('sec', 'dev')), may hold values from -0.09375 to 0.09375
- w_down: bfloat16 [128, 1024, 3584], P(('sec', 'dev')), may hold values from -0.1875 to 0.1875
Outputs:
- expert_out: bfloat16 [4096, 3584], P(('sec', 'dev'))
The draws below stay inside these ranges and needn't reach their ends.
Inputs may be any that keep to these rules, and one draw needn't show every extreme that they name: `expert_ids`: each row names 8 different experts; in the rows of one device no expert is named by more than 4 rows, a bound that some block reaches.
All inputs are finite; a program needn't handle non-finite values.
Results may differ from the reference program's by a relative error of at most 0.0057.
Values may be sent and summed in bfloat16 or wider, within the bound.
A program may use at most 128 MiB of HBM per device.

```python
import math
import jax
import jax.numpy as jnp
import numpy as np
from jax import lax

D = 3584
FF = 1024
TOP = 8
TOK_DEV = 32
EXPERTS = 128
CAP = 4
TOKENS = 4096


def steps_of(key, extent, split, low, top_value):
    gain = 1.0
    for axis_at, shards_of in split:
        steps = jax.random.uniform(jax.random.fold_in(jax.random.fold_in(key, 6), axis_at), (shards_of,), jnp.float32, low / len(split), top_value / len(split))
        gain = gain * jnp.repeat(jnp.exp(steps), extent[axis_at] // shards_of).reshape((-1,) + (1,) * (len(extent) - 1 - axis_at))
    return gain


def shared_out(stream_key, own, number, rows, amount, top, limit, lean):
    sequence = jax.random.permutation(stream_key, amount)
    packed, usual = load_shares(amount, rows * top, limit, lean, True), load_shares(amount, rows * top, limit, lean, False)
    places = jnp.arange(amount)

    def named(sizes, rotation):
        used = int((sizes > 0).sum())
        fixed = max(1, used // 4)
        moved = fixed + (places - fixed + rotation * (used - fixed)) % max(1, amount - fixed)
        return jnp.zeros((amount,), jnp.int32).at[sequence[jnp.where(places < fixed, places, moved)]].set(jnp.asarray(sizes, jnp.int32))

    sizes = jnp.where(number % 4 == 0, named(packed, number // 4), named(usual, number - number // 4 - 1))
    mixed = jax.random.permutation(jax.random.fold_in(own, 3), amount)
    source_of, receiver = mixed[0:amount // 2 * 2:2], mixed[1:amount // 2 * 2:2]
    margin = jnp.minimum(sizes[source_of] - 1, limit - sizes[receiver]) // 2
    margin = jnp.where((source_of == sequence[0]) | (receiver == sequence[0]) | (sizes[receiver] == 0), 0, jnp.maximum(margin, 0))
    moved = jax.random.randint(jax.random.fold_in(own, 4), (amount // 2,), 0, 1 << 20) % (margin + 1)
    sizes = sizes.at[source_of].add(-moved).at[receiver].add(moved)
    items = jnp.searchsorted(jnp.cumsum(sizes), jnp.arange(rows * top), side="right").astype(jnp.int32)
    listing = items.reshape(top, rows).T
    listing = listing[jax.random.permutation(jax.random.fold_in(own, 1), rows)]
    rotation = jax.random.randint(jax.random.fold_in(own, 2), (rows, 1), 0, top)
    return jnp.take_along_axis(listing, (jnp.arange(top)[None, :] + rotation) % top, axis=1)


def load_shares(count, total, most, slope, full):
    portions = [(1 << 20) // math.isqrt(standing ** slope) + 1 for standing in range(1, count + 1)]
    largest = most if full else min(most, max(-(-total // count), total * portions[0] // sum(portions)))
    least = 1 if total - largest >= count - 1 else 0
    holding, spare = [largest] + [least] * (count - 1), total - largest - least * (count - 1)
    while spare > 0:
        movable = [i for i in range(1, count) if holding[i] < largest] or [i for i in range(1, count) if holding[i] < most]
        pool, left = sum([portions[i] for i in movable]), spare
        for i in movable:
            more = min(most - holding[i], max(1, left * portions[i] // pool), spare)
            holding[i] = holding[i] + more
            spare = spare - more
    return np.array(holding)


def bell_draw(own_key, dims, scale, bound, pieces=(), kind=jnp.bfloat16):
    result = jax.random.normal(own_key, dims, jnp.float32) * scale
    if len(pieces) > 0:
        result = steps_of(own_key, dims, pieces, -0.22, 0.18) * result
    return jnp.clip(result, min=-bound, max=bound).astype(kind)


def setup_inputs(seed: int = 0) -> dict:
    streams_of = jax.random.split(jax.random.key(seed), 7)
    tokens = bell_draw(streams_of[0], (TOKENS, D), 1.0, 6.0, ((0, 128),))
    expert_ids_keys = jax.random.split(jax.random.fold_in(streams_of[1], 1), TOKENS // TOK_DEV)
    expert_ids_turns = jax.random.permutation(jax.random.fold_in(streams_of[1], 3), TOKENS // TOK_DEV)
    expert_ids = jax.vmap(lambda own, number: shared_out(jax.random.fold_in(streams_of[1], 2), own, number, TOK_DEV, EXPERTS, TOP, CAP, 2))(expert_ids_keys, expert_ids_turns).reshape((TOKENS, TOP))
    gate_values = jnp.clip(0.1 + 0.5 * jax.random.uniform(streams_of[2], (TOKENS, TOP), jnp.float32) ** steps_of(streams_of[2], (TOKENS, TOP), ((0, 128),), -0.2, 0.2), 0.1, 0.6)
    w_gate = bell_draw(streams_of[3], (EXPERTS, D, FF), D ** -0.5, 0.09375, ((0, 128),))
    w_up = bell_draw(streams_of[4], (EXPERTS, D, FF), D ** -0.5, 0.09375, ((0, 128),))
    w_down = bell_draw(streams_of[5], (EXPERTS, FF, D), FF ** -0.5, 0.1875, ((0, 128),))
    return {"tokens": tokens, "expert_ids": expert_ids, "gate_values": gate_values, "w_gate": w_gate, "w_up": w_up, "w_down": w_down}


def place_slots(expert_ids):
    blocks = TOKENS // TOK_DEV
    flat = expert_ids.reshape(blocks, TOK_DEV * TOP)
    onehot = (flat[:, :, None] == jnp.arange(EXPERTS, dtype=jnp.int32)[None, None, :]).astype(jnp.int32)
    before = jnp.cumsum(onehot, axis=1) - onehot
    slot = jnp.sum(before * onehot, axis=2).astype(jnp.int32)
    return flat, slot


def reference(tokens, expert_ids, gate_values, w_gate, w_up, w_down):
    blocks = TOKENS // TOK_DEV
    flat, slot = place_slots(expert_ids)
    block_of = jnp.broadcast_to(jnp.arange(blocks, dtype=jnp.int32)[:, None], flat.shape)
    token_of = (block_of * TOK_DEV + jnp.arange(TOK_DEV * TOP, dtype=jnp.int32)[None, :] // TOP).astype(jnp.int32)
    table = jnp.full((EXPERTS, blocks, CAP), TOKENS, jnp.int32).at[flat, block_of, slot].set(token_of)
    weights = jnp.zeros((EXPERTS, blocks, CAP), jnp.float32).at[flat, block_of, slot].set(gate_values.reshape(blocks, TOK_DEV * TOP))
    padded = jnp.concatenate([tokens, jnp.zeros((1, D), jnp.bfloat16)], axis=0)

    def step(total, items):
        index_rows, weight_rows, gate_mat, up_mat, down_mat = items
        index_rows = index_rows.reshape(-1)
        rows = padded[index_rows]
        first = jnp.dot(rows, gate_mat, preferred_element_type=jnp.float32)
        second = jnp.dot(rows, up_mat, preferred_element_type=jnp.float32)
        hidden = (jax.nn.silu(first) * second).astype(jnp.bfloat16)
        answer = jnp.dot(hidden, down_mat, preferred_element_type=jnp.float32).astype(jnp.bfloat16)
        total = total.at[index_rows].add(weight_rows.reshape(-1)[:, None] * answer.astype(jnp.float32))
        return total, None

    total, unused = lax.scan(step, jnp.zeros((TOKENS + 1, D), jnp.float32), (table, weights, w_gate, w_up, w_down))
    return total[:TOKENS].astype(jnp.bfloat16)
```

```python
import jax
import jax.numpy as jnp
from jax import lax
from jax.experimental import pallas as pl
from jax.experimental.pallas import tpu as pltpu
from jax.sharding import PartitionSpec as P

MESH = pl.DeviceIdType.MESH
BF = jnp.bfloat16
F32 = jnp.float32
TOK = 32
ROWS = 512
LINE = 128
D = 3584
FF = 1024
ROUNDS = ((512, 384, 384), (384, 384, 512), (384, 384, 256))


def chunks():
    out, start = [], 0
    for widths in ROUNDS:
        row = []
        for width in widths:
            row.append((start, width))
            start += width
        out.append(row)
    return out


def coords():
    z, d = lax.axis_index("sec"), lax.axis_index("dev")
    return z, lax.div(d, 8), lax.rem(lax.div(d, 2), 4), lax.rem(d, 2)


def plane_split(p, co):
    z, x, y, _ = co
    return ((x, y, z), (z, y, x), (z, x, y))[p]


def device_of(p, u, v, j, c):
    z, x, y = ((j, u, v), (u, j, v), (u, v, j))[p]
    return (z, x * 8 + y * 2 + c)


def plane_peer(p, co, n):
    u, v, j = plane_split(p, co)
    un = lax.rem(u + lax.div(n, 8), 4)
    vn = lax.rem(v + lax.rem(lax.div(n, 2), 4), 4)
    cn = lax.rem(co[3] + n, 2)
    return device_of(p, un, vn, j, cn), un * 8 + vn * 2 + cn


def line_peer(p, co, n):
    u, v, j = plane_split(p, co)
    jn = lax.rem(j + n, 4)
    return device_of(p, u, v, jn, co[3]), jn


def iota(shape, dim):
    return lax.broadcasted_iota(jnp.int32, shape, dim)


def dot_nt(a, b):
    return lax.dot_general(a, b, (((1,), (1,)), ((), ())), preferred_element_type=F32)


def dot(a, b):
    return jnp.dot(a, b, preferred_element_type=F32)


def plane_experts(p, co, shape):
    e = lax.shift_right_logical(iota(shape, 0), 4)
    uv, c = lax.shift_right_logical(e, 1), e & 1
    u, v = lax.shift_right_logical(uv, 2), uv & 3
    _, _, j = plane_split(p, co)
    z, x, y = ((j, u, v), (u, j, v), (u, v, j))[p]
    expert = z * 32 + x * 8 + y * 2 + c
    return (iota(shape, 1) == expert).astype(F32).astype(BF)


def reorder(p):
    shape = (ROWS, ROWS)
    r = iota(shape, 0)
    slot, z = r & 3, lax.shift_right_logical(r, 2) & 3
    c, y = lax.shift_right_logical(r, 4) & 1, lax.shift_right_logical(r, 5) & 3
    x = lax.shift_right_logical(r, 7)
    u, v, j = plane_split(p, (z, x, y, c))
    other = (u * 8 + v * 2 + c) * 16 + j * 4 + slot
    return (iota(shape, 1) == other).astype(F32).astype(BF)


def wait_for(ref, sem):
    pltpu.make_async_copy(ref, ref, sem).wait()


def kernel(
    ids_ref, gates_ref, tok_ref, wg_hbm, wu_hbm, wd_hbm, out_ref,
    wg, wu, wd, meta, metas, gath, send, recv, acc_g, acc_u, hid, ans, back, part, fin,
    perm, pick, comb,
    w_sem, meta_ss, meta_rs, s1_ss, s1_rs, s2_ss, s2_rs, s4_ss, s4_rs, s5_ss, s5_rs,
):
    co = coords()
    table = chunks()

    barrier = pltpu.get_barrier_semaphore()
    for p in range(3):
        u, v, j = plane_split(p, co)

        def greet(n, carry, p=p):
            du, dv = lax.div(n, 8), lax.rem(lax.div(n, 2), 4)
            peer, _ = plane_peer(p, co, n)
            if p == 0:
                pl.semaphore_signal(barrier, inc=1, device_id=peer, device_id_type=MESH)
            else:
                fresh = (du != 0) if p == 1 else (du != 0) & (dv != 0)

                @pl.when(fresh)
                def _():
                    pl.semaphore_signal(barrier, inc=1, device_id=peer, device_id_type=MESH)

            return carry

        lax.fori_loop(1, 32, greet, 0)

    weights = [
        pltpu.make_async_copy(src.at[0], dst, w_sem.at[i])
        for i, (src, dst) in enumerate(((wg_hbm, wg), (wu_hbm, wu), (wd_hbm, wd)))
    ]
    for copy in weights:
        copy.start()

    lanes = iota((TOK, 128), 1)
    named = jnp.zeros((TOK, 128), F32)
    gate = jnp.zeros((TOK, 128), F32)
    for k in range(8):
        hit = ids_ref[:, k : k + 1] == lanes
        named = named + hit.astype(F32)
        gate = gate + jnp.where(hit, gates_ref[:, k : k + 1], 0.0)
    earlier = (iota((TOK, TOK), 1) < iota((TOK, TOK), 0)).astype(F32).astype(BF)
    slot = dot(earlier, named.astype(BF))
    gate_hi = gate.astype(BF)
    meta[:, 0:128] = (named * (slot + 1.0)).astype(BF)
    meta[:, 128:256] = gate_hi
    meta[:, 256:384] = (gate - gate_hi.astype(F32)).astype(BF)

    pl.semaphore_wait(barrier, 73)

    for p in range(3):
        _, _, j = plane_split(p, co)
        mine = pl.ds(pl.multiple_of(j * TOK, TOK), TOK)
        pltpu.make_async_copy(meta, metas.at[p, mine], meta_rs.at[p]).start()
        for n in (1, 3, 2):
            peer, _ = line_peer(p, co, n)
            pltpu.make_async_remote_copy(
                meta, metas.at[p, mine], meta_ss, meta_rs.at[p], device_id=peer, device_id_type=MESH
            ).start()
    for r, row in enumerate(table):
        for p, (start, width) in enumerate(row):
            _, _, j = plane_split(p, co)
            mine = pl.ds(pl.multiple_of(j * TOK, TOK), TOK)
            cols = pl.ds(start, width)
            pltpu.make_async_copy(tok_ref.at[:, cols], gath.at[mine, cols], s1_rs.at[r, p]).start()
            for n in (1, 3, 2):
                peer, _ = line_peer(p, co, n)
                pltpu.make_async_remote_copy(
                    tok_ref.at[:, cols], gath.at[mine, cols], s1_ss, s1_rs.at[r, p],
                    device_id=peer, device_id_type=MESH,
                ).start()

    for p in range(3):
        wait_for(metas.at[p], meta_rs.at[p])
        one = plane_experts(p, co, (ROWS, 128))
        code = metas[p, :, 0:128]
        rows, cols = iota((ROWS, LINE), 0), iota((ROWS, LINE), 1)
        want = ((rows & 3) + 1).astype(F32)
        same = (lax.shift_right_logical(rows, 2) & 3) == lax.shift_right_logical(cols, 5)
        pick[p] = jnp.where((dot_nt(one, code) == want) & same, 1.0, 0.0).astype(BF)

    def plane_send(r, src, dst, ss, rs):
        def body(i, carry):
            n = lax.rem(i * 13, 32)
            for p, (start, width) in enumerate(table[r]):
                cols = pl.ds(start, width)
                u, v, _ = plane_split(p, co)
                me = u * 8 + v * 2 + co[3]
                peer, s = plane_peer(p, co, n)
                pltpu.make_async_remote_copy(
                    src.at[pl.ds(pl.multiple_of(s * 16, 16), 16), cols],
                    dst.at[pl.ds(pl.multiple_of(me * 16, 16), 16), cols],
                    ss, rs.at[r, p], device_id=peer, device_id_type=MESH,
                ).start()
            return carry

        lax.fori_loop(1, 32, body, 0)
        for p, (start, width) in enumerate(table[r]):
            u, v, _ = plane_split(p, co)
            mine = pl.ds(pl.multiple_of((u * 8 + v * 2 + co[3]) * 16, 16), 16)
            cols = pl.ds(start, width)
            pltpu.make_async_copy(src.at[mine, cols], dst.at[mine, cols], rs.at[r, p]).start()

    for r, row in enumerate(table):
        for p, (start, width) in enumerate(row):
            cols = pl.ds(start, width)
            wait_for(gath.at[:, cols], s1_rs.at[r, p])
            send[:, cols] = dot(pick[p], gath[:, cols]).astype(BF)
        plane_send(r, send, recv, s2_ss, s2_rs)

    for p in range(3):
        one = plane_experts(p, co, (ROWS, 128))
        rows, cols = iota((LINE, ROWS), 0), iota((LINE, ROWS), 1)
        want = ((cols & 3) + 1).astype(F32)
        same = (lax.shift_right_logical(cols, 2) & 3) == lax.shift_right_logical(rows, 5)
        hit = (dot_nt(metas[p, :, 0:128], one) == want) & same
        comb[p, 0:LINE] = jnp.where(hit, dot_nt(metas[p, :, 128:256], one), 0.0).astype(BF)
        comb[p, LINE : 2 * LINE] = jnp.where(hit, dot_nt(metas[p, :, 256:384], one), 0.0).astype(BF)
    for p in (1, 2):
        perm[p - 1] = reorder(p)

    for copy in weights:
        copy.wait()

    for r, row in enumerate(table):
        for p, (start, width) in enumerate(row):
            cols = pl.ds(start, width)
            wait_for(recv.at[:, cols], s2_rs.at[r, p])
            if p > 0:
                recv[:, cols] = dot(perm[p - 1], recv[:, cols]).astype(BF)
        first = row[0][0]
        depth = pl.ds(first, sum(width for _, width in row))

        def body(i, carry, r=r, depth=depth):
            at = pl.ds(pl.multiple_of(i * 256, 256), 256)
            g = dot(recv[:, depth], wg[depth, at])
            u = dot(recv[:, depth], wu[depth, at])
            if r > 0:
                g = g + acc_g[:, at]
                u = u + acc_u[:, at]
            if r < len(table) - 1:
                acc_g[:, at] = g
                acc_u[:, at] = u
            else:
                hid[0, :, at] = (g / (1.0 + jnp.exp(-g)) * u).astype(BF)
            return carry

        lax.fori_loop(0, FF // 256, body, 0)
    for p in (1, 2):
        hid[p] = lax.dot_general(
            perm[p - 1], hid[0], (((0,), (0,)), ((), ())), preferred_element_type=F32
        ).astype(BF)

    for r, row in enumerate(table):
        for p, (start, width) in enumerate(row):
            cols = pl.ds(start, width)
            ans[:, cols] = dot(hid[p], wd[:, cols]).astype(BF)
        plane_send(r, ans, back, s4_ss, s4_rs)

    for r, row in enumerate(table):
        for p, (start, width) in enumerate(row):
            _, _, j = plane_split(p, co)
            cols = pl.ds(start, width)
            wait_for(back.at[:, cols], s4_rs.at[r, p])
            both = dot(comb[p], back[:, cols])
            part[:, cols] = (both[0:LINE] + both[LINE : 2 * LINE]).astype(BF)
            for n in (1, 3, 2):
                peer, jn = line_peer(p, co, n)
                pltpu.make_async_remote_copy(
                    part.at[pl.ds(pl.multiple_of(jn * TOK, TOK), TOK), cols], fin.at[j, :, cols],
                    s5_ss, s5_rs.at[r, p], device_id=peer, device_id_type=MESH,
                ).start()
            mine = pl.ds(pl.multiple_of(j * TOK, TOK), TOK)
            pltpu.make_async_copy(part.at[mine, cols], fin.at[j, :, cols], s5_rs.at[r, p]).start()

    for r, row in enumerate(table):
        for p, (start, width) in enumerate(row):
            cols = pl.ds(start, width)
            wait_for(fin.at[:, :, cols], s5_rs.at[r, p])
            total = fin[0, :, cols].astype(F32)
            for k in range(1, 4):
                total = total + fin[k, :, cols].astype(F32)
            out_ref[:, cols] = total.astype(BF)

    wait_for(metas.at[:, pl.ds(0, 96)], meta_ss)
    wait_for(gath.at[pl.ds(0, 96)], s1_ss)
    wait_for(send.at[pl.ds(0, 496)], s2_ss)
    wait_for(ans.at[pl.ds(0, 496)], s4_ss)
    wait_for(part.at[pl.ds(0, 96)], s5_ss)


def per_device(tokens, expert_ids, gate_values, w_gate, w_up, w_down):
    n = len(ROUNDS)
    dma = pltpu.SemaphoreType.DMA
    vmem = pl.BlockSpec(memory_space=pltpu.VMEM)
    hbm = pl.BlockSpec(memory_space=pl.ANY)
    return pl.pallas_call(
        kernel,
        out_shape=jax.ShapeDtypeStruct((TOK, D), BF),
        in_specs=[vmem, vmem, vmem, hbm, hbm, hbm],
        out_specs=vmem,
        scratch_shapes=[
            pltpu.VMEM((D, FF), BF),
            pltpu.VMEM((D, FF), BF),
            pltpu.VMEM((FF, D), BF),
            pltpu.VMEM((TOK, 384), BF),
            pltpu.VMEM((3, LINE, 384), BF),
            pltpu.VMEM((LINE, D), BF),
            pltpu.VMEM((ROWS, D), BF),
            pltpu.VMEM((ROWS, D), BF),
            pltpu.VMEM((ROWS, FF), F32),
            pltpu.VMEM((ROWS, FF), F32),
            pltpu.VMEM((3, ROWS, FF), BF),
            pltpu.VMEM((ROWS, D), BF),
            pltpu.VMEM((ROWS, D), BF),
            pltpu.VMEM((LINE, D), BF),
            pltpu.VMEM((4, TOK, D), BF),
            pltpu.VMEM((2, ROWS, ROWS), BF),
            pltpu.VMEM((3, ROWS, LINE), BF),
            pltpu.VMEM((3, 2 * LINE, ROWS), BF),
            dma((3,)),
            dma, dma((3,)),
            dma, dma((n, 3)),
            dma, dma((n, 3)),
            dma, dma((n, 3)),
            dma, dma((n, 3)),
        ],
        compiler_params=pltpu.CompilerParams(
            collective_id=0, has_side_effects=True, vmem_limit_bytes=60 * 2**20
        ),
        cost_estimate=pl.CostEstimate(
            flops=6 * ROWS * D * FF, bytes_accessed=6 * D * FF, transcendentals=ROWS * FF
        ),
        name="expert_layer",
    )(expert_ids, gate_values, tokens, w_gate, w_up, w_down)


def solution(mesh):
    rows = P(("sec", "dev"), None)
    experts = P(("sec", "dev"), None, None)
    return jax.shard_map(
        per_device,
        mesh=mesh,
        in_specs=(rows, rows, rows, experts, experts, experts),
        out_specs=rows,
        check_vma=False,
    )
```

```python
import jax
import jax.numpy as jnp
from jax import lax
from jax.experimental import pallas as pl
from jax.experimental.pallas import tpu as pltpu
from jax.sharding import PartitionSpec as P

MESH = pl.DeviceIdType.MESH
BF = jnp.bfloat16
F32 = jnp.float32
TOK = 32
LINE = 128
ROWS = 512
UNIT = 64
D = 3584
FF = 1024
ROUNDS = ((512, 384, 384), (384, 384, 512), (384, 384, 256))


def chunks():
    out, start = [], 0
    for widths in ROUNDS:
        row = []
        for width in widths:
            row.append((start, width))
            start += width
        out.append(row)
    return out


def coords():
    z, d = lax.axis_index("sec"), lax.axis_index("dev")
    return z, lax.div(d, 8), lax.rem(lax.div(d, 2), 4), lax.rem(d, 2)


def abc(p, zxy):
    return zxy[p], zxy[(p + 1) % 3], zxy[(p + 2) % 3]


def zxy_of(p, a, b, c):
    return ((a, b, c), (c, a, b), (b, c, a))[p]


def device_of(p, a, b, c, core):
    z, x, y = zxy_of(p, a, b, c)
    return (z, x * 8 + y * 2 + core)


def iota(shape, dim):
    return lax.broadcasted_iota(jnp.int32, shape, dim)


def dot_nt(a, b):
    return lax.dot_general(a, b, (((1,), (1,)), ((), ())), preferred_element_type=F32)


def dot(a, b):
    return jnp.dot(a, b, preferred_element_type=F32)


def eye(rows, cols):
    shape = (rows, cols)
    return (iota(shape, 0) == iota(shape, 1)).astype(F32).astype(BF)


def reorder(p):
    shape = (ROWS, ROWS)
    r = iota(shape, 0)
    slot, z, x = r & 3, lax.shift_right_logical(r, 2) & 3, lax.shift_right_logical(r, 4) & 3
    core, y = lax.shift_right_logical(r, 6) & 1, lax.shift_right_logical(r, 7)
    a, b, c = abc(p, (z, x, y))
    other = (c * 2 + core) * UNIT + b * 16 + a * 4 + slot
    return (iota(shape, 1) == other).astype(F32).astype(BF)


def wait_for(ref, sem):
    pltpu.make_async_copy(ref, ref, sem).wait()


def block(i, size):
    return pl.ds(pl.multiple_of(i * size, size), size)


def pair_table(ids_ref, gates_ref):
    ids = ids_ref[...]
    gates = gates_ref[...]
    expert = iota((128, TOK), 0)
    hits = [ids[k : k + 1, :] == expert for k in range(8)]
    named = sum(hit.astype(F32) for hit in hits)
    earlier = (iota((TOK, TOK), 0) < iota((TOK, TOK), 1)).astype(F32).astype(BF)
    slot = dot(named.astype(BF), earlier) + 1.0
    slots = [jnp.sum(jnp.where(hit, slot, 0.0), axis=0, keepdims=True) for hit in hits]
    high = gates.astype(BF).astype(F32)
    lines = [ids.astype(F32)] + slots + [high, gates - high, jnp.zeros((96, TOK), F32)]
    return dot_nt(eye(TOK, TOK), jnp.concatenate(lines, axis=0).astype(BF)).astype(BF)


def kernel(
    ids_ref, gates_ref, tok_ref, wg_hbm, wu_hbm, wd_hbm, out_ref,
    wg, wu, wd, meta, meta1, meta2, gath1, gath2, send, recv, acc_g, acc_u, hid, back, mid, mid_sum, fin,
    perm, pick, comb,
    w_sem, m1_ss, m1_rs, m2_ss, m2_rs, s1_ss, s1_rs, s2_ss, s2_rs, s3_ss, s3_rs,
    s4_ss, s4_rs, s5_ss, s5_rs, s6_ss, s6_rs,
):
    z, x, y, core = coords()
    zxy = (z, x, y)
    table = chunks()
    every = [(r, p, start, width) for r, row in enumerate(table) for p, (start, width) in enumerate(row)]

    barrier = pltpu.get_barrier_semaphore()
    for p in range(3):
        a, b, c = abc(p, zxy)
        for n in (1, 2, 3):
            for other in (0, 1):
                pl.semaphore_signal(
                    barrier, inc=1, device_id=device_of(p, a, b, lax.rem(c + n, 4), lax.rem(core + other, 2)),
                    device_id_type=MESH,
                )
    pl.semaphore_signal(barrier, inc=1, device_id=device_of(0, z, x, y, 1 - core), device_id_type=MESH)

    weights = [
        pltpu.make_async_copy(src.at[0], dst, w_sem.at[i])
        for i, (src, dst) in enumerate(((wg_hbm, wg), (wu_hbm, wu), (wd_hbm, wd)))
    ]
    for copy in weights:
        copy.start()

    meta[...] = pair_table(ids_ref, gates_ref)
    pl.semaphore_wait(barrier, 19)

    def along_a(p, src, dst, ss, rs):
        a, b, c = abc(p, zxy)
        for n in (1, 3, 2):
            to = lax.rem(a + n, 4)
            pltpu.make_async_remote_copy(
                src(to), dst, ss, rs, device_id=device_of(p, to, b, c, core), device_id_type=MESH
            ).start()

    def along_b(p, src, dst, ss, rs):
        a, b, c = abc(p, zxy)
        for n in (1, 3, 2):
            to = lax.rem(b + n, 4)
            pltpu.make_async_remote_copy(
                src(to), dst, ss, rs, device_id=device_of(p, a, to, c, core), device_id_type=MESH
            ).start()

    def along_c(p, src, dst, cols, ss, rs):
        a, b, c = abc(p, zxy)
        mine = block(c * 2 + core, UNIT)
        for n in (1, 3, 2, 0):
            for m in (0, 1):
                if n == 0 and m == 0:
                    continue
                to, to_core = lax.rem(c + n, 4), lax.rem(core + m, 2)
                pltpu.make_async_remote_copy(
                    src.at[block(to * 2 + to_core, UNIT), cols], dst.at[mine, cols], ss, rs,
                    device_id=device_of(p, a, b, to, to_core), device_id_type=MESH,
                ).start()
        pltpu.make_async_copy(src.at[mine, cols], dst.at[mine, cols], rs).start()

    for p in range(3):
        mine = block(zxy[p], TOK)
        along_a(p, lambda to: meta, meta1.at[p, mine], m1_ss, m1_rs.at[p])
        pltpu.make_async_copy(meta, meta1.at[p, mine], m1_rs.at[p]).start()
    for r, p, start, width in every:
        cols, mine = pl.ds(start, width), block(zxy[p], TOK)
        along_a(p, lambda to: tok_ref.at[:, cols], gath1.at[mine, cols], s1_ss, s1_rs.at[r, p])
        pltpu.make_async_copy(tok_ref.at[:, cols], gath1.at[mine, cols], s1_rs.at[r, p]).start()
    for p in range(3):
        mine = block(zxy[(p + 1) % 3], LINE)
        wait_for(meta1.at[p], m1_rs.at[p])
        along_b(p, lambda to: meta1.at[p], meta2.at[p, mine], m2_ss, m2_rs.at[p])
        pltpu.make_async_copy(meta1.at[p], meta2.at[p, mine], m2_rs.at[p]).start()
    for r, p, start, width in every:
        cols, mine = pl.ds(start, width), block(zxy[(p + 1) % 3], LINE)
        wait_for(gath1.at[:, cols], s1_rs.at[r, p])
        along_b(p, lambda to: gath1.at[:, cols], gath2.at[mine, cols], s2_ss, s2_rs.at[r, p])
        pltpu.make_async_copy(gath1.at[:, cols], gath2.at[mine, cols], s2_rs.at[r, p]).start()

    def tables(p, weighted):
        a, b, c = abc(p, zxy)
        lanes = dot_nt(eye(TOK, 128), meta2[p])
        ids, slots, high, low = (lanes[8 * i : 8 * i + 8] for i in range(4))

        def per_unit(values):
            out = []
            for u in range(8):
                to_z, to_x, to_y = zxy_of(p, a, b, u // 2)
                expert = to_z * 32 + to_x * 8 + to_y * 2 + u % 2
                hit = ids == expert.astype(F32)
                row = jnp.sum(jnp.where(hit, values, 0.0), axis=0, keepdims=True)
                out.append(jnp.broadcast_to(row, (UNIT, ROWS)))
            return jnp.concatenate(out, axis=0)

        rows, cols = iota((ROWS, ROWS), 0), iota((ROWS, ROWS), 1)
        want = ((rows & 3) + 1).astype(F32)
        same = (lax.shift_right_logical(rows, 2) & 15) == lax.shift_right_logical(cols, 5)
        hit = (per_unit(slots) == want) & same
        if weighted:
            comb[p, 0:ROWS] = jnp.where(hit, per_unit(high), 0.0).T.astype(BF)
            comb[p, ROWS : 2 * ROWS] = jnp.where(hit, per_unit(low), 0.0).T.astype(BF)
        else:
            pick[p] = jnp.where(hit, 1.0, 0.0).astype(BF)

    for p in range(3):
        wait_for(meta2.at[p], m2_rs.at[p])
        tables(p, False)
    for r, p, start, width in every:
        cols = pl.ds(start, width)
        wait_for(gath2.at[:, cols], s2_rs.at[r, p])
        send[:, cols] = dot(pick[p], gath2[:, cols]).astype(BF)
        along_c(p, send, recv, cols, s3_ss, s3_rs.at[r, p])

    for p in (1, 2):
        perm[p - 1] = reorder(p)
    for p in range(3):
        tables(p, True)
    for copy in weights:
        copy.wait()

    for r, row in enumerate(table):
        for p, (start, width) in enumerate(row):
            cols = pl.ds(start, width)
            wait_for(recv.at[:, cols], s3_rs.at[r, p])
            if p > 0:
                recv[:, cols] = dot(perm[p - 1], recv[:, cols]).astype(BF)
        first = row[0][0]
        depth = pl.ds(first, sum(width for _, width in row))

        def body(i, carry, r=r, depth=depth):
            at = block(i, 256)
            g = dot(recv[:, depth], wg[depth, at])
            u = dot(recv[:, depth], wu[depth, at])
            if r > 0:
                g = g + acc_g[:, at]
                u = u + acc_u[:, at]
            if r < len(table) - 1:
                acc_g[:, at] = g
                acc_u[:, at] = u
            else:
                hid[0, :, at] = (g / (1.0 + jnp.exp(-g)) * u).astype(BF)
            return carry

        lax.fori_loop(0, FF // 256, body, 0)
    for p in (1, 2):
        hid[p] = lax.dot_general(
            perm[p - 1], hid[0], (((0,), (0,)), ((), ())), preferred_element_type=F32
        ).astype(BF)

    wait_for(send.at[pl.ds(0, ROWS - UNIT)], s3_ss)
    for r, p, start, width in every:
        cols = pl.ds(start, width)
        send[:, cols] = dot(hid[p], wd[:, cols]).astype(BF)
        along_c(p, send, back, cols, s4_ss, s4_rs.at[r, p])
    for r, p, start, width in every:
        cols, b = pl.ds(start, width), zxy[(p + 1) % 3]
        wait_for(back.at[:, cols], s4_rs.at[r, p])
        both = dot(comb[p], back[:, cols])
        recv[:, cols] = (both[0:ROWS] + both[ROWS : 2 * ROWS]).astype(BF)
        along_b(p, lambda to: recv.at[block(to, LINE), cols], mid.at[b, :, cols], s5_ss, s5_rs.at[r, p])
        pltpu.make_async_copy(recv.at[block(b, LINE), cols], mid.at[b, :, cols], s5_rs.at[r, p]).start()
    for r, p, start, width in every:
        cols, a = pl.ds(start, width), zxy[p]
        wait_for(mid.at[:, :, cols], s5_rs.at[r, p])
        mid_sum[:, cols] = sum(mid[k, :, cols].astype(F32) for k in range(4)).astype(BF)
        along_a(p, lambda to: mid_sum.at[block(to, TOK), cols], fin.at[a, :, cols], s6_ss, s6_rs.at[r, p])
        pltpu.make_async_copy(mid_sum.at[block(a, TOK), cols], fin.at[a, :, cols], s6_rs.at[r, p]).start()
    for r, p, start, width in every:
        cols = pl.ds(start, width)
        wait_for(fin.at[:, :, cols], s6_rs.at[r, p])
        out_ref[:, cols] = sum(fin[k, :, cols].astype(F32) for k in range(4)).astype(BF)

    wait_for(meta1.at[:, pl.ds(0, 96)], m1_ss)
    wait_for(meta2.at[:, pl.ds(0, 384)], m2_ss)
    wait_for(gath1.at[pl.ds(0, 96)], s1_ss)
    wait_for(gath2.at[pl.ds(0, 384)], s2_ss)
    wait_for(send.at[pl.ds(0, ROWS - UNIT)], s4_ss)
    wait_for(recv.at[pl.ds(0, 384)], s5_ss)
    wait_for(mid_sum.at[pl.ds(0, 96)], s6_ss)


def per_device(tokens, expert_ids, gate_values, w_gate, w_up, w_down):
    n = len(ROUNDS)
    dma = pltpu.SemaphoreType.DMA
    vmem = pl.BlockSpec(memory_space=pltpu.VMEM)
    hbm = pl.BlockSpec(memory_space=pl.ANY)
    return pl.pallas_call(
        kernel,
        out_shape=jax.ShapeDtypeStruct((TOK, D), BF),
        in_specs=[vmem, vmem, vmem, hbm, hbm, hbm],
        out_specs=vmem,
        scratch_shapes=[
            pltpu.VMEM((D, FF), BF),
            pltpu.VMEM((D, FF), BF),
            pltpu.VMEM((FF, D), BF),
            pltpu.VMEM((TOK, 128), BF),
            pltpu.VMEM((3, LINE, 128), BF),
            pltpu.VMEM((3, ROWS, 128), BF),
            pltpu.VMEM((LINE, D), BF),
            pltpu.VMEM((ROWS, D), BF),
            pltpu.VMEM((ROWS, D), BF),
            pltpu.VMEM((ROWS, D), BF),
            pltpu.VMEM((ROWS, FF), F32),
            pltpu.VMEM((ROWS, FF), F32),
            pltpu.VMEM((3, ROWS, FF), BF),
            pltpu.VMEM((ROWS, D), BF),
            pltpu.VMEM((4, LINE, D), BF),
            pltpu.VMEM((LINE, D), BF),
            pltpu.VMEM((4, TOK, D), BF),
            pltpu.VMEM((2, ROWS, ROWS), BF),
            pltpu.VMEM((3, ROWS, ROWS), BF),
            pltpu.VMEM((3, 2 * ROWS, ROWS), BF),
            dma((3,)),
            dma, dma((3,)),
            dma, dma((3,)),
            dma, dma((n, 3)),
            dma, dma((n, 3)),
            dma, dma((n, 3)),
            dma, dma((n, 3)),
            dma, dma((n, 3)),
            dma, dma((n, 3)),
        ],
        compiler_params=pltpu.CompilerParams(
            collective_id=0, has_side_effects=True, vmem_limit_bytes=62 * 2**20
        ),
        cost_estimate=pl.CostEstimate(
            flops=6 * ROWS * D * FF, bytes_accessed=6 * D * FF, transcendentals=ROWS * FF
        ),
        name="expert_layer",
    )(expert_ids.T, gate_values.T, tokens, w_gate, w_up, w_down)


def solution(mesh):
    rows = P(("sec", "dev"), None)
    experts = P(("sec", "dev"), None, None)
    return jax.shard_map(
        per_device,
        mesh=mesh,
        in_specs=(rows, rows, rows, experts, experts, experts),
        out_specs=rows,
        check_vma=False,
    )
```

```python
import jax
import jax.numpy as jnp
from jax import lax
from jax.experimental import pallas as pl
from jax.experimental.pallas import tpu as pltpu
from jax.sharding import PartitionSpec as P

MESH = pl.DeviceIdType.MESH
BF = jnp.bfloat16
F32 = jnp.float32
TOK = 32
LINE = 128
ROWS = 512
UNIT = 64
D = 3584
FF = 1024
ROUNDS = ((256, 256, 256), (256, 256, 256), (256, 256, 256), (256, 256, 256), (256, 128, 128))


def chunks():
    out, start = [], 0
    for widths in ROUNDS:
        row = []
        for width in widths:
            row.append((start, width))
            start += width
        out.append(row)
    return out


def coords():
    z, d = lax.axis_index("sec"), lax.axis_index("dev")
    return z, lax.div(d, 8), lax.rem(lax.div(d, 2), 4), lax.rem(d, 2)


def abc(p, zxy):
    return zxy[p], zxy[(p + 1) % 3], zxy[(p + 2) % 3]


def zxy_of(p, a, b, c):
    return ((a, b, c), (c, a, b), (b, c, a))[p]


def device_of(p, a, b, c, core):
    z, x, y = zxy_of(p, a, b, c)
    return (z, x * 8 + y * 2 + core)


def iota(shape, dim):
    return lax.broadcasted_iota(jnp.int32, shape, dim)


def dot_nt(a, b):
    return lax.dot_general(a, b, (((1,), (1,)), ((), ())), preferred_element_type=F32)


def dot(a, b):
    return jnp.dot(a, b, preferred_element_type=F32)


def eye(rows, cols):
    shape = (rows, cols)
    return (iota(shape, 0) == iota(shape, 1)).astype(F32).astype(BF)


def reorder(p):
    shape = (ROWS, ROWS)
    r = iota(shape, 0)
    slot, z, x = r & 3, lax.shift_right_logical(r, 2) & 3, lax.shift_right_logical(r, 4) & 3
    core, y = lax.shift_right_logical(r, 6) & 1, lax.shift_right_logical(r, 7)
    a, b, c = abc(p, (z, x, y))
    other = (c * 2 + core) * UNIT + b * 16 + a * 4 + slot
    return (iota(shape, 1) == other).astype(F32).astype(BF)


def wait_for(ref, sem):
    pltpu.make_async_copy(ref, ref, sem).wait()


def block(i, size):
    return pl.ds(pl.multiple_of(i * size, size), size)


def pair_table(ids_ref, gates_ref):
    ids = ids_ref[...]
    gates = gates_ref[...]
    expert = iota((128, TOK), 0)
    hits = [ids[k : k + 1, :] == expert for k in range(8)]
    named = sum(hit.astype(F32) for hit in hits)
    earlier = (iota((TOK, TOK), 0) < iota((TOK, TOK), 1)).astype(F32).astype(BF)
    slot = dot(named.astype(BF), earlier) + 1.0
    slots = [jnp.sum(jnp.where(hit, slot, 0.0), axis=0, keepdims=True) for hit in hits]
    lines = [ids.astype(F32)] + slots + [gates, jnp.zeros((104, TOK), F32)]
    return dot_nt(eye(TOK, TOK), jnp.concatenate(lines, axis=0).astype(BF)).astype(BF)


def kernel(
    ids_ref, gates_ref, tok_ref, wg_hbm, wu_hbm, wd_hbm, out_ref,
    wg, wu, wd, meta, meta1, meta2, gath1, gath2, send, recv, acc_g, acc_u, hid, back, far, mid, mid_sum, fin,
    perm, pick, comb,
    w_sem, m1_ss, m1_rs, m2_ss, m2_rs, s1_ss, s1_rs, s2_ss, s2_rs, s3_ss, s3_rs,
    s4_ss, s4_rs, s5_ss, s5_rs, s6_ss, s6_rs, s7_ss, s7_rs, s8_ss, s8_rs,
):
    z, x, y, core = coords()
    zxy = (z, x, y)
    table = chunks()
    rounds = len(table)

    def parts_of(r):
        return [(p, start, pl.ds(start, width)) for p, (start, width) in enumerate(table[r])]


    barrier = pltpu.get_barrier_semaphore()
    for p in range(3):
        a, b, c = abc(p, zxy)
        for n in (1, 2, 3):
            for other in (0, 1):
                pl.semaphore_signal(
                    barrier, inc=1, device_id=device_of(p, a, b, lax.rem(c + n, 4), lax.rem(core + other, 2)),
                    device_id_type=MESH,
                )
    pl.semaphore_signal(barrier, inc=1, device_id=device_of(0, z, x, y, 1 - core), device_id_type=MESH)

    weights = [
        pltpu.make_async_copy(src.at[0], dst, w_sem.at[i])
        for i, (src, dst) in enumerate(((wg_hbm, wg), (wu_hbm, wu), (wd_hbm, wd)))
    ]
    for copy in weights:
        copy.start()

    meta[...] = pair_table(ids_ref, gates_ref)
    for p in (1, 2):
        perm[p - 1] = reorder(p)
    pl.semaphore_wait(barrier, 19)

    def along_a(p, src, dst, ss, rs):
        a, b, c = abc(p, zxy)
        for n in (1, 3, 2):
            to = lax.rem(a + n, 4)
            pltpu.make_async_remote_copy(
                src(to), dst, ss, rs, device_id=device_of(p, to, b, c, core), device_id_type=MESH
            ).start()

    def next_b(p, step, src, dst, ss, rs):
        a, b, c = abc(p, zxy)
        pltpu.make_async_remote_copy(
            src, dst, ss, rs, device_id=device_of(p, a, lax.rem(b + step, 4), c, core), device_id_type=MESH
        ).start()

    def along_c(p, src, dst, cols, ss, rs):
        a, b, c = abc(p, zxy)
        mine = block(c * 2 + core, UNIT)
        for n in (1, 3, 2, 0):
            for m in (0, 1):
                if n == 0 and m == 0:
                    continue
                to, to_core = lax.rem(c + n, 4), lax.rem(core + m, 2)
                pltpu.make_async_remote_copy(
                    src.at[block(to * 2 + to_core, UNIT), cols], dst.at[mine, cols], ss, rs,
                    device_id=device_of(p, a, b, to, to_core), device_id_type=MESH,
                ).start()
        pltpu.make_async_copy(src.at[mine, cols], dst.at[mine, cols], rs).start()

    for p in range(3):
        mine = block(zxy[p], TOK)
        along_a(p, lambda to: meta, meta1.at[p, mine], m1_ss, m1_rs.at[p])
        pltpu.make_async_copy(meta, meta1.at[p, mine], m1_rs.at[p]).start()
    for r in range(rounds):
        for p, start, cols in parts_of(r):
            mine = block(zxy[p], TOK)
            along_a(p, lambda to: tok_ref.at[:, cols], gath1.at[mine, cols], s1_ss, s1_rs.at[r, p])
            pltpu.make_async_copy(tok_ref.at[:, cols], gath1.at[mine, cols], s1_rs.at[r, p]).start()
    for p in range(3):
        b = zxy[(p + 1) % 3]
        wait_for(meta1.at[p], m1_rs.at[p])
        for n in (1, 3, 2):
            next_b(p, n, meta1.at[p], meta2.at[p, block(b, LINE)], m2_ss, m2_rs.at[p])
        pltpu.make_async_copy(meta1.at[p], meta2.at[p, block(b, LINE)], m2_rs.at[p]).start()

    def to_neighbours(r):
        for p, start, cols in parts_of(r):
            mine = block(zxy[(p + 1) % 3], LINE)
            wait_for(gath1.at[:, cols], s1_rs.at[r, p])
            next_b(p, 1, gath1.at[:, cols], gath2.at[mine, cols], s2_ss, s2_rs.at[r, p, 0])
            next_b(p, 3, gath1.at[:, cols], gath2.at[mine, cols], s2_ss, s2_rs.at[r, p, 1])
            pltpu.make_async_copy(gath1.at[:, cols], gath2.at[mine, cols], s7_rs.at[r, p]).start()

    def pass_on(r):
        for p, start, cols in parts_of(r):
            b = zxy[(p + 1) % 3]
            for side, step, source in ((0, 1, lax.rem(b + 3, 4)), (1, 3, lax.rem(b + 1, 4))):
                wait_for(gath2.at[block(source, LINE), cols], s2_rs.at[r, p, side])
                half = gath2.at[block(source * 2 + side, 64), cols]
                next_b(p, step, half, half, s7_ss, s7_rs.at[r, p])

    def tables(p, weighted):
        a, b, c = abc(p, zxy)
        lanes = dot_nt(eye(TOK, 128), meta2[p])
        ids, slots, gates = (lanes[8 * i : 8 * i + 8] for i in range(3))

        def per_unit(values):
            out = []
            for u in range(8):
                to_z, to_x, to_y = zxy_of(p, a, b, u // 2)
                expert = to_z * 32 + to_x * 8 + to_y * 2 + u % 2
                hit = ids == expert.astype(F32)
                row = jnp.sum(jnp.where(hit, values, 0.0), axis=0, keepdims=True)
                out.append(jnp.broadcast_to(row, (UNIT, ROWS)))
            return jnp.concatenate(out, axis=0)

        rows, cols = iota((ROWS, ROWS), 0), iota((ROWS, ROWS), 1)
        want = ((rows & 3) + 1).astype(F32)
        same = (lax.shift_right_logical(rows, 2) & 15) == lax.shift_right_logical(cols, 5)
        hit = (per_unit(slots) == want) & same
        if weighted:
            comb[p] = jnp.where(hit, per_unit(gates), 0.0).T.astype(BF)
        else:
            pick[p] = jnp.where(hit, 1.0, 0.0).astype(BF)

    def slots_out(r):
        for p, start, cols in parts_of(r):
            if r == 0:
                wait_for(meta2.at[p], m2_rs.at[p])
                tables(p, False)
            wait_for(gath2.at[pl.ds(0, 2 * LINE), cols], s7_rs.at[r, p])
            send[:, cols] = dot(pick[p], gath2[:, cols]).astype(BF)
            along_c(p, send, recv, cols, s3_ss, s3_rs.at[r, p])
        if r < 3:
            tables(r, True)

    def multiply(r):
        if r == 0:
            for copy in weights:
                copy.wait()
        for p, start, cols in parts_of(r):
            wait_for(recv.at[:, cols], s3_rs.at[r, p])
            if p > 0:
                recv[:, cols] = dot(perm[p - 1], recv[:, cols]).astype(BF)
        depth = pl.ds(table[r][0][0], sum(width for _, width in table[r]))
        for i in range(FF // 512):
            at = pl.ds(i * 512, 512)
            g = dot(recv[:, depth], wg[depth, at])
            u = dot(recv[:, depth], wu[depth, at])
            if r > 0:
                g = g + acc_g[:, at]
                u = u + acc_u[:, at]
            if r < rounds - 1:
                acc_g[:, at] = g
                acc_u[:, at] = u
            else:
                hid[0, :, at] = (g / (1.0 + jnp.exp(-g)) * u).astype(BF)

    def answers_out(r):
        for p, start, cols in parts_of(r):
            if r == 0 and p > 0:
                hid[p] = lax.dot_general(
                    perm[p - 1], hid[0], (((0,), (0,)), ((), ())), preferred_element_type=F32
                ).astype(BF)
            send[:, cols] = dot(hid[p], wd[:, cols]).astype(BF)
            along_c(p, send, back, cols, s4_ss, s4_rs.at[r, p])

    def sums_out(r):
        for p, start, cols in parts_of(r):
            across = lax.rem(zxy[(p + 1) % 3] + 2, 4)
            wait_for(back.at[:, cols], s4_rs.at[r, p])
            recv[:, cols] = dot(comb[p], back[:, cols]).astype(BF)
            for side, step in ((0, 1), (1, 3)):
                half = recv.at[block(across * 2 + side, 64), cols]
                next_b(p, step, half, far.at[side, :, cols], s5_ss, s5_rs.at[r, p])

    def sums_on(r):
        for p, start, cols in parts_of(r):
            b = zxy[(p + 1) % 3]
            wait_for(far.at[:, :, cols], s5_rs.at[r, p])
            for side, step in ((0, 1), (1, 3)):
                to = lax.rem(b + step, 4)
                half = block(to * 2 + side, 64)
                recv[half, cols] = (recv[half, cols].astype(F32) + far[side, :, cols].astype(F32)).astype(BF)
                next_b(p, step, recv.at[block(to, LINE), cols], mid.at[side, :, cols], s8_ss, s8_rs.at[r, p])

    def sums_home(r):
        for p, start, cols in parts_of(r):
            a, b, _ = abc(p, zxy)
            wait_for(mid.at[:, :, cols], s8_rs.at[r, p])
            total = recv[block(b, LINE), cols].astype(F32)
            mid_sum[:, cols] = (total + mid[0, :, cols].astype(F32) + mid[1, :, cols].astype(F32)).astype(BF)
            along_a(p, lambda to: mid_sum.at[block(to, TOK), cols], fin.at[a, :, cols], s6_ss, s6_rs.at[r, p])
            pltpu.make_async_copy(mid_sum.at[block(a, TOK), cols], fin.at[a, :, cols], s6_rs.at[r, p]).start()

    def finish(r):
        for p, start, cols in parts_of(r):
            wait_for(fin.at[:, :, cols], s6_rs.at[r, p])
            out_ref[:, cols] = sum(fin[k, :, cols].astype(F32) for k in range(4)).astype(BF)

    def staggered(*steps):
        for i in range(rounds + max(lag for _, lag in steps)):
            for step, lag in steps:
                if 0 <= i - lag < rounds:
                    step(i - lag)

    staggered((to_neighbours, 0), (pass_on, 2), (slots_out, 4), (multiply, 6))
    wait_for(send.at[pl.ds(0, ROWS - UNIT)], s3_ss)
    staggered((answers_out, 0), (sums_out, 2), (sums_on, 4), (sums_home, 6), (finish, 8))

    wait_for(meta1.at[:, pl.ds(0, 96)], m1_ss)
    wait_for(meta2.at[:, pl.ds(0, 384)], m2_ss)
    wait_for(gath1.at[pl.ds(0, 96)], s1_ss)
    wait_for(gath2.at[pl.ds(0, 256)], s2_ss)
    wait_for(gath2.at[pl.ds(0, 128)], s7_ss)
    wait_for(send.at[pl.ds(0, ROWS - UNIT)], s4_ss)
    wait_for(recv.at[pl.ds(0, 128)], s5_ss)
    wait_for(recv.at[pl.ds(0, 256)], s8_ss)
    wait_for(mid_sum.at[pl.ds(0, 96)], s6_ss)


def per_device(tokens, expert_ids, gate_values, w_gate, w_up, w_down):
    n = len(ROUNDS)
    dma = pltpu.SemaphoreType.DMA
    vmem = pl.BlockSpec(memory_space=pltpu.VMEM)
    hbm = pl.BlockSpec(memory_space=pl.ANY)
    return pl.pallas_call(
        kernel,
        out_shape=jax.ShapeDtypeStruct((TOK, D), BF),
        in_specs=[vmem, vmem, vmem, hbm, hbm, hbm],
        out_specs=vmem,
        scratch_shapes=[
            pltpu.VMEM((D, FF), BF),
            pltpu.VMEM((D, FF), BF),
            pltpu.VMEM((FF, D), BF),
            pltpu.VMEM((TOK, 128), BF),
            pltpu.VMEM((3, LINE, 128), BF),
            pltpu.VMEM((3, ROWS, 128), BF),
            pltpu.VMEM((LINE, D), BF),
            pltpu.VMEM((ROWS, D), BF),
            pltpu.VMEM((ROWS, D), BF),
            pltpu.VMEM((ROWS, D), BF),
            pltpu.VMEM((ROWS, FF), F32),
            pltpu.VMEM((ROWS, FF), F32),
            pltpu.VMEM((3, ROWS, FF), BF),
            pltpu.VMEM((ROWS, D), BF),
            pltpu.VMEM((2, 64, D), BF),
            pltpu.VMEM((2, LINE, D), BF),
            pltpu.VMEM((LINE, D), BF),
            pltpu.VMEM((4, TOK, D), BF),
            pltpu.VMEM((2, ROWS, ROWS), BF),
            pltpu.VMEM((3, ROWS, ROWS), BF),
            pltpu.VMEM((3, ROWS, ROWS), BF),
            dma((3,)),
            dma, dma((3,)),
            dma, dma((3,)),
            dma, dma((n, 3)),
            dma, dma((n, 3, 2)),
            dma, dma((n, 3)),
            dma, dma((n, 3)),
            dma, dma((n, 3)),
            dma, dma((n, 3)),
            dma, dma((n, 3)),
            dma, dma((n, 3)),
        ],
        compiler_params=pltpu.CompilerParams(
            collective_id=0, has_side_effects=True, vmem_limit_bytes=62 * 2**20
        ),
        cost_estimate=pl.CostEstimate(
            flops=6 * ROWS * D * FF, bytes_accessed=6 * D * FF, transcendentals=ROWS * FF
        ),
        name="expert_layer",
    )(expert_ids.T, gate_values.T, tokens, w_gate, w_up, w_down)


def solution(mesh):
    rows = P(("sec", "dev"), None)
    experts = P(("sec", "dev"), None, None)
    return jax.shard_map(
        per_device,
        mesh=mesh,
        in_specs=(rows, rows, rows, experts, experts, experts),
        out_specs=rows,
        check_vma=False,
    )
```

```python
import jax
import jax.numpy as jnp
from jax import lax
from jax.experimental import pallas as pl
from jax.experimental.pallas import tpu as pltpu
from jax.sharding import PartitionSpec as P

MESH = pl.DeviceIdType.MESH
BF = jnp.bfloat16
F32 = jnp.float32
TOK = 32
LINE = 128
ROWS = 512
UNIT = 64
D = 3584
FF = 1024
ROUNDS = ((256, 256, 256), (512, 256, 256), (256, 384, 384), (256, 256, 256))


def chunks():
    out, start = [], 0
    for widths in ROUNDS:
        row = []
        for width in widths:
            row.append((start, width))
            start += width
        out.append(row)
    return out


def coords():
    z, d = lax.axis_index("sec"), lax.axis_index("dev")
    return z, lax.div(d, 8), lax.rem(lax.div(d, 2), 4), lax.rem(d, 2)


def abc(p, zxy):
    return zxy[p], zxy[(p + 1) % 3], zxy[(p + 2) % 3]


def zxy_of(p, a, b, c):
    return ((a, b, c), (c, a, b), (b, c, a))[p]


def device_of(p, a, b, c, core):
    z, x, y = zxy_of(p, a, b, c)
    return (z, x * 8 + y * 2 + core)


def iota(shape, dim):
    return lax.broadcasted_iota(jnp.int32, shape, dim)


def dot_nt(a, b):
    return lax.dot_general(a, b, (((1,), (1,)), ((), ())), preferred_element_type=F32)


def dot(a, b):
    return jnp.dot(a, b, preferred_element_type=F32)


def eye(rows, cols):
    shape = (rows, cols)
    return (iota(shape, 0) == iota(shape, 1)).astype(F32).astype(BF)


def reorder(p):
    shape = (ROWS, ROWS)
    r = iota(shape, 0)
    slot, z, x = r & 3, lax.shift_right_logical(r, 2) & 3, lax.shift_right_logical(r, 4) & 3
    core, y = lax.shift_right_logical(r, 6) & 1, lax.shift_right_logical(r, 7)
    a, b, c = abc(p, (z, x, y))
    other = (c * 2 + core) * UNIT + b * 16 + a * 4 + slot
    return (iota(shape, 1) == other).astype(F32).astype(BF)


def wait_for(ref, sem):
    pltpu.make_async_copy(ref, ref, sem).wait()


def block(i, size):
    return pl.ds(pl.multiple_of(i * size, size), size)


def pair_table(ids_ref, gates_ref):
    ids = ids_ref[...]
    gates = gates_ref[...]
    expert = iota((128, TOK), 0)
    hits = [ids[k : k + 1, :] == expert for k in range(8)]
    named = sum(hit.astype(F32) for hit in hits)
    earlier = (iota((TOK, TOK), 0) < iota((TOK, TOK), 1)).astype(F32).astype(BF)
    slot = dot(named.astype(BF), earlier) + 1.0
    slots = [jnp.sum(jnp.where(hit, slot, 0.0), axis=0, keepdims=True) for hit in hits]
    lines = [ids.astype(F32)] + slots + [gates, jnp.zeros((104, TOK), F32)]
    return dot_nt(eye(TOK, TOK), jnp.concatenate(lines, axis=0).astype(BF)).astype(BF)


def kernel(
    ids_ref, gates_ref, tok_ref, wg_hbm, wu_hbm, wd_hbm, out_ref,
    wg, wu, wd, meta, meta1, meta2, gath1, gath2, send, recv, acc_g, acc_u, hid, back, far, mid, mid_sum, fin,
    perm, pick, comb,
    w_sem, m1_ss, m1_rs, m2_ss, m2_rs, s1_ss, s1_rs, s2_ss, s2_rs, s3_ss, s3_rs,
    s4_ss, s4_rs, s5_ss, s5_rs, s6_ss, s6_rs, s7_ss, s7_rs, s8_ss, s8_rs,
):
    z, x, y, core = coords()
    zxy = (z, x, y)
    table = chunks()
    rounds = len(table)

    def parts_of(r):
        return [(p, start, pl.ds(start, width)) for p, (start, width) in enumerate(table[r])]


    barrier = pltpu.get_barrier_semaphore()
    for p in range(3):
        a, b, c = abc(p, zxy)
        for n in (1, 2, 3):
            for other in (0, 1):
                pl.semaphore_signal(
                    barrier, inc=1, device_id=device_of(p, a, b, lax.rem(c + n, 4), lax.rem(core + other, 2)),
                    device_id_type=MESH,
                )
    pl.semaphore_signal(barrier, inc=1, device_id=device_of(0, z, x, y, 1 - core), device_id_type=MESH)

    weights = [
        pltpu.make_async_copy(src.at[0], dst, w_sem.at[i])
        for i, (src, dst) in enumerate(((wg_hbm, wg), (wu_hbm, wu), (wd_hbm, wd)))
    ]
    for copy in weights:
        copy.start()

    meta[...] = pair_table(ids_ref, gates_ref)
    for p in (1, 2):
        perm[p - 1] = reorder(p)
    pl.semaphore_wait(barrier, 19)

    def along_a(p, src, dst, ss, rs):
        a, b, c = abc(p, zxy)
        for n in (1, 3, 2):
            to = lax.rem(a + n, 4)
            pltpu.make_async_remote_copy(
                src(to), dst, ss, rs, device_id=device_of(p, to, b, c, core), device_id_type=MESH
            ).start()

    def next_b(p, step, src, dst, ss, rs):
        a, b, c = abc(p, zxy)
        pltpu.make_async_remote_copy(
            src, dst, ss, rs, device_id=device_of(p, a, lax.rem(b + step, 4), c, core), device_id_type=MESH
        ).start()

    def along_c(p, src, dst, cols, ss, rs):
        a, b, c = abc(p, zxy)
        mine = block(c * 2 + core, UNIT)
        for n in (1, 3, 2, 0):
            for m in (0, 1):
                if n == 0 and m == 0:
                    continue
                to, to_core = lax.rem(c + n, 4), lax.rem(core + m, 2)
                pltpu.make_async_remote_copy(
                    src.at[block(to * 2 + to_core, UNIT), cols], dst.at[mine, cols], ss, rs,
                    device_id=device_of(p, a, b, to, to_core), device_id_type=MESH,
                ).start()
        pltpu.make_async_copy(src.at[mine, cols], dst.at[mine, cols], rs).start()

    for p in range(3):
        mine = block(zxy[p], TOK)
        along_a(p, lambda to: meta, meta1.at[p, mine], m1_ss, m1_rs.at[p])
        pltpu.make_async_copy(meta, meta1.at[p, mine], m1_rs.at[p]).start()
    for r in range(rounds):
        for p, start, cols in parts_of(r):
            mine = block(zxy[p], TOK)
            along_a(p, lambda to: tok_ref.at[:, cols], gath1.at[mine, cols], s1_ss, s1_rs.at[r, p])
            pltpu.make_async_copy(tok_ref.at[:, cols], gath1.at[mine, cols], s1_rs.at[r, p]).start()
    for p in range(3):
        b = zxy[(p + 1) % 3]
        wait_for(meta1.at[p], m1_rs.at[p])
        for n in (1, 3, 2):
            next_b(p, n, meta1.at[p], meta2.at[p, block(b, LINE)], m2_ss, m2_rs.at[p])
        pltpu.make_async_copy(meta1.at[p], meta2.at[p, block(b, LINE)], m2_rs.at[p]).start()

    def to_neighbours(r):
        for p, start, cols in parts_of(r):
            mine = block(zxy[(p + 1) % 3], LINE)
            wait_for(gath1.at[:, cols], s1_rs.at[r, p])
            next_b(p, 1, gath1.at[:, cols], gath2.at[mine, cols], s2_ss, s2_rs.at[r, p, 0])
            next_b(p, 3, gath1.at[:, cols], gath2.at[mine, cols], s2_ss, s2_rs.at[r, p, 1])
            pltpu.make_async_copy(gath1.at[:, cols], gath2.at[mine, cols], s7_rs.at[r, p]).start()

    def pass_on(r):
        for p, start, cols in parts_of(r):
            b = zxy[(p + 1) % 3]
            for side, step, source in ((0, 1, lax.rem(b + 3, 4)), (1, 3, lax.rem(b + 1, 4))):
                wait_for(gath2.at[block(source, LINE), cols], s2_rs.at[r, p, side])
                half = gath2.at[block(source * 2 + side, 64), cols]
                next_b(p, step, half, half, s7_ss, s7_rs.at[r, p])

    def tables(p, weighted):
        a, b, c = abc(p, zxy)
        lanes = dot_nt(eye(TOK, 128), meta2[p])
        ids, slots, gates = (lanes[8 * i : 8 * i + 8] for i in range(3))

        def per_unit(values):
            out = []
            for u in range(8):
                to_z, to_x, to_y = zxy_of(p, a, b, u // 2)
                expert = to_z * 32 + to_x * 8 + to_y * 2 + u % 2
                hit = ids == expert.astype(F32)
                row = jnp.sum(jnp.where(hit, values, 0.0), axis=0, keepdims=True)
                out.append(jnp.broadcast_to(row, (UNIT, ROWS)))
            return jnp.concatenate(out, axis=0)

        rows, cols = iota((ROWS, ROWS), 0), iota((ROWS, ROWS), 1)
        want = ((rows & 3) + 1).astype(F32)
        same = (lax.shift_right_logical(rows, 2) & 15) == lax.shift_right_logical(cols, 5)
        hit = (per_unit(slots) == want) & same
        if weighted:
            comb[p] = jnp.where(hit, per_unit(gates), 0.0).T.astype(BF)
        else:
            pick[p] = jnp.where(hit, 1.0, 0.0).astype(BF)

    def slots_out(r):
        for p, start, cols in parts_of(r):
            if r == 0:
                wait_for(meta2.at[p], m2_rs.at[p])
                tables(p, False)
            wait_for(gath2.at[pl.ds(0, 2 * LINE), cols], s7_rs.at[r, p])
            send[:, cols] = dot(pick[p], gath2[:, cols]).astype(BF)
            along_c(p, send, recv, cols, s3_ss, s3_rs.at[r, p])
        if r < 3:
            tables(r, True)

    def multiply(r):
        if r == 0:
            for copy in weights:
                copy.wait()
        for p, start, cols in parts_of(r):
            wait_for(recv.at[:, cols], s3_rs.at[r, p])
            if p > 0:
                recv[:, cols] = dot(perm[p - 1], recv[:, cols]).astype(BF)
        depth = pl.ds(table[r][0][0], sum(width for _, width in table[r]))
        for i in range(FF // 512):
            at = pl.ds(i * 512, 512)
            g = dot(recv[:, depth], wg[depth, at])
            u = dot(recv[:, depth], wu[depth, at])
            if r > 0:
                g = g + acc_g[:, at]
                u = u + acc_u[:, at]
            if r < rounds - 1:
                acc_g[:, at] = g
                acc_u[:, at] = u
            else:
                hid[0, :, at] = (g / (1.0 + jnp.exp(-g)) * u).astype(BF)

    def answers_out(r):
        for p, start, cols in parts_of(r):
            if r == 0 and p > 0:
                hid[p] = lax.dot_general(
                    perm[p - 1], hid[0], (((0,), (0,)), ((), ())), preferred_element_type=F32
                ).astype(BF)
            send[:, cols] = dot(hid[p], wd[:, cols]).astype(BF)
            along_c(p, send, back, cols, s4_ss, s4_rs.at[r, p])

    def sums_out(r):
        for p, start, cols in parts_of(r):
            across = lax.rem(zxy[(p + 1) % 3] + 2, 4)
            wait_for(back.at[:, cols], s4_rs.at[r, p])
            recv[:, cols] = dot(comb[p], back[:, cols]).astype(BF)
            for side, step in ((0, 1), (1, 3)):
                half = recv.at[block(across * 2 + side, 64), cols]
                next_b(p, step, half, far.at[side, :, cols], s5_ss, s5_rs.at[r, p])

    def sums_on(r):
        for p, start, cols in parts_of(r):
            b = zxy[(p + 1) % 3]
            wait_for(far.at[:, :, cols], s5_rs.at[r, p])
            for side, step in ((0, 1), (1, 3)):
                to = lax.rem(b + step, 4)
                half = block(to * 2 + side, 64)
                recv[half, cols] = (recv[half, cols].astype(F32) + far[side, :, cols].astype(F32)).astype(BF)
                next_b(p, step, recv.at[block(to, LINE), cols], mid.at[side, :, cols], s8_ss, s8_rs.at[r, p])

    def sums_home(r):
        for p, start, cols in parts_of(r):
            a, b, _ = abc(p, zxy)
            wait_for(mid.at[:, :, cols], s8_rs.at[r, p])
            total = recv[block(b, LINE), cols].astype(F32)
            mid_sum[:, cols] = (total + mid[0, :, cols].astype(F32) + mid[1, :, cols].astype(F32)).astype(BF)
            along_a(p, lambda to: mid_sum.at[block(to, TOK), cols], fin.at[a, :, cols], s6_ss, s6_rs.at[r, p])
            pltpu.make_async_copy(mid_sum.at[block(a, TOK), cols], fin.at[a, :, cols], s6_rs.at[r, p]).start()

    def finish(r):
        for p, start, cols in parts_of(r):
            wait_for(fin.at[:, :, cols], s6_rs.at[r, p])
            out_ref[:, cols] = sum(fin[k, :, cols].astype(F32) for k in range(4)).astype(BF)

    def staggered(*steps):
        for i in range(rounds + max(lag for _, lag in steps)):
            for step, lag in steps:
                if 0 <= i - lag < rounds:
                    step(i - lag)

    staggered((to_neighbours, 0), (pass_on, 2), (slots_out, 4), (multiply, 6))
    wait_for(send.at[pl.ds(0, ROWS - UNIT)], s3_ss)
    staggered((answers_out, 0), (sums_out, 2), (sums_on, 4), (sums_home, 6), (finish, 8))

    wait_for(meta1.at[:, pl.ds(0, 96)], m1_ss)
    wait_for(meta2.at[:, pl.ds(0, 384)], m2_ss)
    wait_for(gath1.at[pl.ds(0, 96)], s1_ss)
    wait_for(gath2.at[pl.ds(0, 256)], s2_ss)
    wait_for(gath2.at[pl.ds(0, 128)], s7_ss)
    wait_for(send.at[pl.ds(0, ROWS - UNIT)], s4_ss)
    wait_for(recv.at[pl.ds(0, 128)], s5_ss)
    wait_for(recv.at[pl.ds(0, 256)], s8_ss)
    wait_for(mid_sum.at[pl.ds(0, 96)], s6_ss)


def per_device(tokens, expert_ids, gate_values, w_gate, w_up, w_down):
    n = len(ROUNDS)
    dma = pltpu.SemaphoreType.DMA
    vmem = pl.BlockSpec(memory_space=pltpu.VMEM)
    hbm = pl.BlockSpec(memory_space=pl.ANY)
    return pl.pallas_call(
        kernel,
        out_shape=jax.ShapeDtypeStruct((TOK, D), BF),
        in_specs=[vmem, vmem, vmem, hbm, hbm, hbm],
        out_specs=vmem,
        scratch_shapes=[
            pltpu.VMEM((D, FF), BF),
            pltpu.VMEM((D, FF), BF),
            pltpu.VMEM((FF, D), BF),
            pltpu.VMEM((TOK, 128), BF),
            pltpu.VMEM((3, LINE, 128), BF),
            pltpu.VMEM((3, ROWS, 128), BF),
            pltpu.VMEM((LINE, D), BF),
            pltpu.VMEM((ROWS, D), BF),
            pltpu.VMEM((ROWS, D), BF),
            pltpu.VMEM((ROWS, D), BF),
            pltpu.VMEM((ROWS, FF), F32),
            pltpu.VMEM((ROWS, FF), F32),
            pltpu.VMEM((3, ROWS, FF), BF),
            pltpu.VMEM((ROWS, D), BF),
            pltpu.VMEM((2, 64, D), BF),
            pltpu.VMEM((2, LINE, D), BF),
            pltpu.VMEM((LINE, D), BF),
            pltpu.VMEM((4, TOK, D), BF),
            pltpu.VMEM((2, ROWS, ROWS), BF),
            pltpu.VMEM((3, ROWS, ROWS), BF),
            pltpu.VMEM((3, ROWS, ROWS), BF),
            dma((3,)),
            dma, dma((3,)),
            dma, dma((3,)),
            dma, dma((n, 3)),
            dma, dma((n, 3, 2)),
            dma, dma((n, 3)),
            dma, dma((n, 3)),
            dma, dma((n, 3)),
            dma, dma((n, 3)),
            dma, dma((n, 3)),
            dma, dma((n, 3)),
        ],
        compiler_params=pltpu.CompilerParams(
            collective_id=0, has_side_effects=True, vmem_limit_bytes=62 * 2**20
        ),
        cost_estimate=pl.CostEstimate(
            flops=6 * ROWS * D * FF, bytes_accessed=6 * D * FF, transcendentals=ROWS * FF
        ),
        name="expert_layer",
    )(expert_ids.T, gate_values.T, tokens, w_gate, w_up, w_down)


def solution(mesh):
    rows = P(("sec", "dev"), None)
    experts = P(("sec", "dev"), None, None)
    return jax.shard_map(
        per_device,
        mesh=mesh,
        in_specs=(rows, rows, rows, experts, experts, experts),
        out_specs=rows,
        check_vma=False,
    )
```
